32 devices in a mesh: groups: 2 (over y), dap: 4 (over z), seq: 2 (over x), chan: 2 (over core).
Axes of the slice: x: 2, y: 2, z: 4, core: 2. Of those that a mesh axis runs over, the one named last changes fastest.
Arguments:
- alignment: bfloat16 [128, 96, 256], P(('groups', 'seq'), 'dap'), parts along dimension 0, may hold values from -8 to 8
- align_mask: int32 [128, 96], P('groups'), parts along dimension 0, may hold values from 0 to 1, as said below
- pair_mask: int32 [192, 96], P(('groups', 'dap')), parts along dimension 0, may hold values 0 or 1
- cotangent: bfloat16 [192, 96, 128], P(('groups', 'dap'), 'seq', 'chan'), parts along dimension 0, may hold values from -150 to 150
- left_weight: bfloat16 [256, 32], replicated, may hold values from -0.375 to 0.375
- right_weight: bfloat16 [256, 32], replicated, may hold values from -0.375 to 0.375
- out_weight: bfloat16 [1024, 128], P(None, 'chan'), may hold values from -0.1875 to 0.1875
Outputs:
- pair_update: bfloat16 [192, 96, 128], P(('groups', 'dap'), 'seq', 'chan'), parts along dimension 0
- grad_alignment: bfloat16 [128, 96, 256], P(('groups', 'seq'), 'dap'), parts along dimension 0
- grad_left_weight: float32 [512, 32], P('groups'), parts along dimension 0
- grad_right_weight: float32 [512, 32], P('groups'), parts along dimension 0
- grad_out_weight: float32 [2048, 128], P('groups', 'chan'), parts along dimension 0
The draws below stay inside these ranges and needn't reach their ends.
There are 2 independent parts, one for each index of `groups`. The reference program is written for one: setup_inputs(seed, part) draws one part's arguments, and reference() takes and returns one part's arrays. A program takes and returns all parts, laid end to end along the dimension named above; an argument that names none is the same for every part. Nothing has to cross between parts.
Inputs may be any that keep to these rules, and one draw needn't show every extreme that they name: `align_mask`: entries are 0 or 1; the first sequence is 1 at every residue.
All inputs are finite; a program needn't handle non-finite values. No bound on the sum of `pair_mask` on one device may be relied on, other than what follows from the above.
Results may differ from the reference program's by a relative error of at most 0.0075.
Values may be sent and summed in bfloat16 or wider, within the bound.
A program may use at most 64 MiB of HBM per device.

```python
import jax
import jax.numpy as jnp
from jax import lax

CM = 256
CO = 32
CZ = 128
RES_DEV = 24
SBLK = 32
RES = 96
SEQS = 64


def draw_alignment(key, part):
    key = jax.random.fold_in(key, 11)
    profile_key, jitter_key = jax.random.split(key)
    profile = jax.random.normal(profile_key, (1, RES, CM), jnp.float32)
    jitter = jax.random.normal(jitter_key, (SEQS, RES, CM), jnp.float32)
    return jnp.clip(profile + jitter, -8.0, 8.0).astype(jnp.bfloat16)


def draw_align_mask(key, part):
    key = jax.random.fold_in(key, 23)
    rate_key, entry_key = jax.random.split(key)
    keep_rates = jax.random.randint(rate_key, (SEQS, 1), 55, 100)
    entries = jax.random.randint(entry_key, (SEQS, RES), 0, 100)
    kept_mask = (entries < keep_rates).astype(jnp.int32)
    return kept_mask.at[0].set(1)


def plant(array, stream_key, smallest, largest):
    longest = array.shape.index(max(array.shape))
    spots = []
    for shift in (0, 1):
        where = [jax.random.randint(jax.random.fold_in(stream_key, axis), (), 0, length) for axis, length in enumerate(array.shape)]
        where[longest] = (where[longest] + shift) % array.shape[longest]
        spots.append(tuple(where))
    return array.at[spots[0]].set(smallest).at[spots[1]].set(largest)


def block_levels(rng, shape, pieces, smallest, largest):
    def one(position, parts):
        draws = jax.random.uniform(jax.random.fold_in(jax.random.fold_in(rng, 6), position), (parts,), jnp.float32, smallest / len(pieces), largest / len(pieces))
        return jnp.repeat(jnp.exp(draws), shape[position] // parts).reshape((-1,) + (1,) * (len(shape) - position - 1))

    loudness = one(*pieces[0])
    for cut in pieces[1:]:
        loudness = loudness * one(*cut)
    return loudness


def normal_values(key, dims, scale, most, cuts=(), kind=jnp.bfloat16):
    factor_of = block_levels(key, dims, cuts, -0.22, 0.18) if cuts else 1.0
    result = jax.random.normal(key, dims, jnp.float32) * scale * factor_of
    return jnp.minimum(jnp.maximum(result, -most), most).astype(kind)


def setup_inputs(seed: int = 0, part: int = 0) -> dict:
    key_list = jax.random.split(jax.random.key(seed), 8)
    part_splits = jax.random.split(jax.random.fold_in(key_list[7], part), 8)
    return {
        "alignment": draw_alignment(jax.random.fold_in(jax.random.fold_in(key_list[7], part), 71), part),
        "align_mask": draw_align_mask(jax.random.fold_in(jax.random.fold_in(key_list[7], part), 71), part),
        "pair_mask": plant((jax.random.randint(part_splits[2], (RES, RES), 0, 8) < 7).astype(jnp.int32), jax.random.fold_in(part_splits[2], 1), 0, 1),
        "cotangent": normal_values(part_splits[3], (RES, RES, CZ), 25.0, 150.0, ((0, 4), (1, 2), (2, 2))),
        "left_weight": normal_values(key_list[4], (CM, CO), CM ** -0.5, 0.375),
        "right_weight": normal_values(key_list[5], (CM, CO), CM ** -0.5, 0.375),
        "out_weight": normal_values(key_list[6], (CO * CO, CZ), (CO * CO) ** -0.5, 0.1875, ((1, 2),)),
    }


def layer_norm(values):
    center = values - lax.optimization_barrier(jnp.mean(values, axis=-1, keepdims=True))
    variance = lax.optimization_barrier(jnp.mean(center * center, axis=-1, keepdims=True))
    return center * lax.rsqrt(variance + 1e-05)

def reference(alignment, align_mask, pair_mask, cotangent, left_weight, right_weight, out_weight):
    source = alignment.astype(jnp.float32)
    normed = layer_norm(source).astype(jnp.bfloat16)
    normed_float = normed.astype(jnp.float32)
    mask_float = align_mask.astype(jnp.float32)
    left_proj = jnp.einsum('src,cd->srd', normed_float, left_weight.astype(jnp.float32))
    right_proj = jnp.einsum('src,cd->srd', normed_float, right_weight.astype(jnp.float32))
    left_act = (mask_float[:, :, None] * left_proj).astype(jnp.bfloat16)
    right_act = (mask_float[:, :, None] * right_proj).astype(jnp.bfloat16)
    counts = jnp.dot(mask_float.T, mask_float, precision=lax.Precision.HIGHEST)
    pair_scale = pair_mask.astype(jnp.float32) / (counts + 0.001)
    num_blocks = SEQS // SBLK
    left_blocks = left_act.astype(jnp.float32).reshape(num_blocks, SBLK, RES, CO)
    right_blocks = right_act.astype(jnp.float32).reshape(num_blocks, SBLK, RES, CO)
    scaled_grad = (cotangent.astype(jnp.float32) * pair_scale[:, :, None]).astype(jnp.bfloat16)
    out_float = out_weight.astype(jnp.float32)

    def row_step(running, row_index):
        wo_acc, right_acc = running
        offset = (row_index * RES_DEV).astype(jnp.int32)
        left_rows = lax.dynamic_slice_in_dim(left_blocks, offset, RES_DEV, 2)
        outer_prod = jnp.einsum('ksic,ksjd->kijcd', left_rows, right_blocks).astype(jnp.bfloat16)
        outer_prod = outer_prod.reshape(num_blocks, RES_DEV, RES, CO * CO).astype(jnp.float32)
        projected = jnp.einsum('kijf,fe->ije', outer_prod, out_float)
        scale_rows = lax.dynamic_slice_in_dim(pair_scale, offset, RES_DEV, 0)
        pair_rows = (projected * scale_rows[:, :, None]).astype(jnp.bfloat16)
        grad_rows = lax.dynamic_slice_in_dim(scaled_grad, offset, RES_DEV, 0).astype(jnp.float32)
        wo_term = jnp.einsum('kijf,ije->fe', outer_prod, grad_rows)
        douter = jnp.einsum('ije,fe->ijf', grad_rows, out_float).astype(jnp.bfloat16)
        douter = douter.astype(jnp.float32).reshape(RES_DEV, RES, CO, CO)
        left_term = jnp.einsum('ijcd,ksjd->ksic', douter, right_blocks)
        right_term = jnp.einsum('ijcd,ksic->ksjd', douter, left_rows)
        return ((wo_acc + wo_term, right_acc + right_term), (pair_rows, left_term))
    initial = (jnp.zeros((CO * CO, CZ), jnp.float32), jnp.zeros((num_blocks, SBLK, RES, CO), jnp.float32))
    (wo_sum, right_sum), (pair_parts, left_parts) = lax.scan(row_step, initial, jnp.arange(RES // RES_DEV, dtype=jnp.int32))
    pair_update = pair_parts.reshape(RES, RES, CZ)
    left_raw = jnp.transpose(left_parts, (1, 2, 0, 3, 4)).reshape(SEQS, RES, CO)
    left_grad = (mask_float[:, :, None] * left_raw).astype(jnp.bfloat16)
    right_grad = (mask_float[:, :, None] * right_sum.reshape(SEQS, RES, CO)).astype(jnp.bfloat16)
    left_float = left_grad.astype(jnp.float32)
    right_float = right_grad.astype(jnp.float32)
    grad_left_weight = jnp.einsum('src,srd->cd', normed_float, left_float) / RES
    grad_right_weight = jnp.einsum('src,srd->cd', normed_float, right_float) / RES
    normed_grad = jnp.einsum('srd,cd->src', left_float, left_weight.astype(jnp.float32))
    normed_grad = normed_grad + jnp.einsum('srd,cd->src', right_float, right_weight.astype(jnp.float32))
    _, pullback = jax.vjp(layer_norm, source)
    grad_alignment = pullback(normed_grad)[0].astype(jnp.bfloat16)
    return (pair_update, grad_alignment, grad_left_weight, grad_right_weight, wo_sum / RES)
```

```python
import functools

import jax
import jax.numpy as jnp
from jax import lax
from jax.experimental import pallas as pl
from jax.experimental.pallas import tpu as pltpu
from jax.sharding import PartitionSpec as P

MESH = pl.DeviceIdType.MESH
VMEM_BYTES = 48 * 1024 * 1024
F32 = jnp.float32
BF16 = jnp.bfloat16


def layer_norm(values):
    center = values - jnp.mean(values, axis=-1, keepdims=True)
    variance = jnp.mean(center * center, axis=-1, keepdims=True)
    return center * lax.rsqrt(variance + 1e-05)


def dot(a, b, ca, cb):
    return lax.dot_general(a, b, (((ca,), (cb,)), ((), ())), preferred_element_type=F32)


def vmem_call(kernel, out_shape, scratch, num_in, collective_id=None):
    params = dict(vmem_limit_bytes=VMEM_BYTES)
    if collective_id is not None:
        params.update(collective_id=collective_id, has_side_effects=True)
    return pl.pallas_call(
        kernel,
        out_shape=out_shape,
        in_specs=[pl.BlockSpec(memory_space=pltpu.VMEM)] * num_in,
        out_specs=jax.tree.map(lambda _: pl.BlockSpec(memory_space=pltpu.VMEM), out_shape),
        scratch_shapes=scratch,
        compiler_params=pltpu.CompilerParams(**params),
    )


def plane_barrier(dap, seq):
    num = dap * seq
    me = lax.axis_index("dap") * seq + lax.axis_index("seq")
    barrier = pltpu.get_barrier_semaphore()
    for step in range(1, num):
        peer = lax.rem(me + step, num)
        pl.semaphore_signal(
            barrier,
            inc=1,
            device_id={"dap": peer // seq, "seq": lax.rem(peer, seq)},
            device_id_type=MESH,
        )
    return barrier, num - 1


def gather_kernel(dap, seq, left_ref, right_ref, lall_ref, rall_ref, lbuf, rbuf, lsend, lrecv, rsend, rrecv):
    per = dap // seq
    a = lax.axis_index("dap")
    q = lax.axis_index("seq")
    barrier, count = plane_barrier(dap, seq)
    pl.semaphore_wait(barrier, count)

    def right_copy(step):
        return pltpu.make_async_remote_copy(
            src_ref=right_ref,
            dst_ref=rbuf.at[lax.rem(a, per), q],
            send_sem=rsend.at[step],
            recv_sem=rrecv.at[lax.rem(a, per), q],
            device_id={"dap": lax.rem(a + step, dap), "seq": a // per},
            device_id_type=MESH,
        )

    def left_copy(step):
        return pltpu.make_async_remote_copy(
            src_ref=left_ref,
            dst_ref=lbuf.at[q],
            send_sem=lsend.at[step],
            recv_sem=lrecv.at[q],
            device_id={"seq": lax.rem(q + step, seq)},
            device_id_type=MESH,
        )

    own = a // per == q
    for step in range(1, dap):
        right_copy(step).start()
    pl.when(jnp.logical_not(own))(lambda: right_copy(0).start())
    for step in range(1, seq):
        left_copy(step).start()
    for src_q in range(seq):

        @pl.when(src_q != q)
        def _():
            pltpu.make_async_copy(lbuf.at[src_q], lbuf.at[src_q], lrecv.at[src_q]).wait()
            lall_ref[src_q] = lbuf[src_q]

        @pl.when(src_q == q)
        def _():
            lall_ref[src_q] = left_ref[...]

        for block in range(per):
            mine = jnp.logical_and(q * per + block == a, src_q == q)

            @pl.when(jnp.logical_not(mine))
            def _():
                pltpu.make_async_copy(
                    rbuf.at[block, src_q], rbuf.at[block, src_q], rrecv.at[block, src_q]
                ).wait()
                rall_ref[block, src_q] = rbuf[block, src_q]

            @pl.when(mine)
            def _():
                rall_ref[block, src_q] = right_ref[...]

    for step in range(1, dap):
        right_copy(step).wait_send()
    pl.when(jnp.logical_not(own))(lambda: right_copy(0).wait_send())
    for step in range(1, seq):
        left_copy(step).wait_send()


def main_kernel(left_ref, rt_ref, w_ref, cot_ref, sct_ref, pu_ref, dl_ref, drt_ref, dw_ref, sg, wbd, outer, dout):
    rows, cols, chan = cot_ref.shape
    width = 32
    pack = 128 // width
    groups = rows // pack
    for g in range(groups):
        parts = [
            cot_ref[g * pack + k].astype(F32) * sct_ref[:, g * pack + k : g * pack + k + 1]
            for k in range(pack)
        ]
        sg[g * cols : (g + 1) * cols, :] = jnp.concatenate(parts, axis=1).astype(BF16)
    row_part = lax.broadcasted_iota(jnp.int32, (128, pack * chan), 0) // width
    lane_part = lax.broadcasted_iota(jnp.int32, (128, pack * chan), 1) // chan
    diagonal = (row_part == lane_part).astype(F32).astype(BF16)
    for d in range(width):
        block = w_ref[d * width : (d + 1) * width, :]
        block = jnp.concatenate([block] * pack, axis=1)
        wbd[d * 128 : (d + 1) * 128, :] = jnp.concatenate([block] * pack, axis=0) * diagonal
    for ch in range(width // 8):
        piece = dot(sg[...], wbd[ch * 1024 : (ch + 1) * 1024, :], 1, 1).astype(BF16)
        for dd in range(8):
            at = (ch * 8 + dd) * cols
            for g in range(groups):
                dout[at : at + cols, g * 128 : (g + 1) * 128] = piece[
                    g * cols : (g + 1) * cols, dd * 128 : (dd + 1) * 128
                ]
    dl_ref[...] = dot(rt_ref[...], dout[...], 1, 0).astype(BF16)
    drt_ref[...] = dot(left_ref[...], dout[...], 1, 1).astype(BF16)
    for ch in range(width // 8):
        piece = dot(rt_ref[:, ch * 8 * cols : (ch + 1) * 8 * cols], left_ref[...], 0, 0)
        piece = piece.astype(BF16)
        for dd in range(8):
            at = (ch * 8 + dd) * 128
            for g in range(groups):
                outer[g * cols : (g + 1) * cols, at : at + 128] = piece[
                    dd * cols : (dd + 1) * cols, g * 128 : (g + 1) * 128
                ]
    lane_of = lax.broadcasted_iota(jnp.int32, (chan, 128), 1) // width
    for ch in range(width // pack):
        wide = dot(sg[...], outer[:, ch * pack * 128 : (ch + 1) * pack * 128], 0, 0)
        total = jnp.zeros((chan, 128), F32)
        for d in range(pack):
            part = jnp.zeros((chan, 128), F32)
            for k in range(pack):
                part = jnp.where(
                    lane_of == k,
                    wide[k * chan : (k + 1) * chan, d * 128 : (d + 1) * 128],
                    part,
                )
            part = part + pltpu.roll(part, 64, 1)
            part = part + pltpu.roll(part, 32, 1)
            total = jnp.where(lane_of == d, part, total)
        dw_ref[ch] = total.astype(BF16)
    projected = dot(outer[...], wbd[...], 1, 0)
    for g in range(groups):
        for k in range(pack):
            i = g * pack + k
            pu_ref[i] = (
                projected[g * cols : (g + 1) * cols, k * chan : (k + 1) * chan]
                * sct_ref[:, i : i + 1]
            ).astype(BF16)


def reduce_kernel(
    dap, seq, dl_ref, dr_ref, wo_ref, lg_ref, rg_ref, wot_ref,
    l1, r1, l2, r2, lin, rin, pair, wrecv, wall,
    csend, crecv, lsend, lrecv, rsend, rrecv, wsend, wrsem, gsend, grecv,
):
    per = dap // seq
    num = dap * seq
    a = lax.axis_index("dap")
    q = lax.axis_index("seq")
    h = lax.axis_index("chan")
    other = 1 - h
    me = a * seq + q
    barrier, count = plane_barrier(dap, seq)
    pl.semaphore_signal(barrier, inc=1, device_id={"chan": other}, device_id_type=MESH)
    pl.semaphore_wait(barrier, count + 1)

    def core_copy(src, dst, sem):
        return pltpu.make_async_remote_copy(
            src_ref=src, dst_ref=dst, send_sem=csend.at[sem], recv_sem=crecv.at[sem],
            device_id={"chan": other}, device_id_type=MESH,
        )

    def plane_copy(src, dst, send, recv, peer_a, peer_q):
        return pltpu.make_async_remote_copy(
            src_ref=src, dst_ref=dst, send_sem=send, recv_sem=recv,
            device_id={"dap": peer_a, "seq": peer_q}, device_id_type=MESH,
        )

    left_core = core_copy(dl_ref.at[other], l1, 0)
    right_core = core_copy(dr_ref.at[other], r1, 1)
    left_core.start()
    right_core.start()

    def scatter(step):
        peer = lax.rem(me + step, num)
        return plane_copy(
            wo_ref.at[peer], wrecv.at[step], wsend.at[step], wrsem.at[step],
            peer // seq, lax.rem(peer, seq),
        )

    def regather(step):
        peer = lax.rem(me + step, num)
        return plane_copy(
            wall.at[me], wall.at[me], gsend.at[step], grecv.at[me],
            peer // seq, lax.rem(peer, seq),
        )

    for step in range(1, num):
        scatter(step).start()

    def left_out(dest_q):
        return plane_copy(l2.at[dest_q], lin.at[q], lsend.at[dest_q], lrecv.at[q], a, dest_q)

    def right_out(block, dest_q):
        return plane_copy(
            r2.at[block, dest_q], rin.at[a], rsend.at[block, dest_q], rrecv.at[a],
            q * per + block, dest_q,
        )

    def is_me(block, dest_q):
        return jnp.logical_and(q * per + block == a, dest_q == q)

    right_core.wait()
    for block in range(per):
        for dest_q in range(seq):
            r2[block, dest_q] = (
                dr_ref[h, block, dest_q].astype(F32) + r1[block, dest_q].astype(F32)
            ).astype(BF16)

            @pl.when(jnp.logical_not(is_me(block, dest_q)))
            def _():
                right_out(block, dest_q).start()

    left_core.wait()
    for dest_q in range(seq):
        l2[dest_q] = (dl_ref[h, dest_q].astype(F32) + l1[dest_q].astype(F32)).astype(BF16)

        @pl.when(dest_q != q)
        def _():
            left_out(dest_q).start()

    def arrived(buf, sem):
        pltpu.make_async_copy(buf, buf, sem).wait()

    left_sum = l2[q].astype(F32)
    for step in range(1, seq):
        src_q = lax.rem(q + step, seq)
        arrived(lin.at[src_q], lrecv.at[src_q])
        left_sum = left_sum + lin[src_q].astype(F32)
    pair[h, 0] = left_sum.astype(BF16)

    own = a // per == q

    @pl.when(own)
    def _():
        rin[a] = r2[lax.rem(a, per), q]

    @pl.when(jnp.logical_not(own))
    def _():
        arrived(rin.at[a], rrecv.at[a])

    right_sum = rin[a].astype(F32)
    for step in range(1, dap):
        src_a = lax.rem(a + step, dap)
        arrived(rin.at[src_a], rrecv.at[src_a])
        right_sum = right_sum + rin[src_a].astype(F32)
    pair[h, 1] = right_sum.astype(BF16)
    final = core_copy(pair.at[h], pair.at[h], 2)
    final.start()

    wo_sum = wo_ref[me].astype(F32)
    for step in range(1, num):
        arrived(wrecv.at[step], wrsem.at[step])
        wo_sum = wo_sum + wrecv[step].astype(F32)
    wall[me] = wo_sum.astype(BF16)
    for step in range(1, num):
        regather(step).start()

    final.wait_send()
    arrived(pair.at[other], crecv.at[2])
    for half in range(2):
        lg_ref[half] = pair[half, 0]
        rg_ref[half] = pair[half, 1]
    for step in range(1, num):
        src = lax.rem(me + step, num)
        arrived(wall.at[src], grecv.at[src])
    wot_ref[...] = wall[...]

    for step in range(1, num):
        scatter(step).wait_send()
        regather(step).wait_send()
    for dest_q in range(seq):

        @pl.when(dest_q != q)
        def _():
            left_out(dest_q).wait_send()

        for block in range(per):

            @pl.when(jnp.logical_not(is_me(block, dest_q)))
            def _():
                right_out(block, dest_q).wait_send()


def total_kernel(dap, seq, part_ref, total_ref, own, inbox, send, recv):
    num = dap * seq
    me = lax.axis_index("dap") * seq + lax.axis_index("seq")
    barrier, count = plane_barrier(dap, seq)
    own[...] = part_ref[...].astype(BF16)
    pl.semaphore_wait(barrier, count)

    def copy(step):
        peer = lax.rem(me + step, num)
        return pltpu.make_async_remote_copy(
            src_ref=own, dst_ref=inbox.at[step], send_sem=send.at[step], recv_sem=recv.at[step],
            device_id={"dap": peer // seq, "seq": lax.rem(peer, seq)}, device_id_type=MESH,
        )

    for step in range(1, num):
        copy(step).start()
    inbox[0] = own[...]
    for step in range(1, num):
        copy(step).wait()
    total = jnp.zeros(part_ref.shape, F32)
    for source in range(num):
        total = total + inbox[lax.rem(me - source + num, num)].astype(F32)
    total_ref[...] = total


def body(alignment, align_mask, pair_mask, cotangent, left_weight, right_weight, out_weight):
    seqs, rows, chans = alignment.shape
    width = left_weight.shape[1]
    chan = out_weight.shape[1]
    dap, seq = lax.axis_size("dap"), lax.axis_size("seq")
    per, num = dap // seq, dap * seq
    total_res, all_seqs = rows * dap, seqs * seq
    cols = total_res // seq
    a, q = lax.axis_index("dap"), lax.axis_index("seq")
    half = seqs // 2
    flat = rows * width

    mask_bf = align_mask.astype(BF16)
    own_mask = lax.dynamic_slice(align_mask, (q * seqs, a * rows), (seqs, rows)).astype(F32)
    mask_rows = lax.dynamic_slice_in_dim(mask_bf, a * rows, rows, 1)
    mask_cols = lax.dynamic_slice_in_dim(mask_bf, q * cols, cols, 1)
    counts = dot(mask_cols, mask_rows, 0, 0)
    own_pairs = lax.dynamic_slice_in_dim(pair_mask, q * cols, cols, 1)
    scale_t = own_pairs.T.astype(F32) / (counts + 0.001)

    source = alignment.astype(F32)
    normed = layer_norm(source).astype(BF16)
    both_weights = jnp.concatenate([left_weight, right_weight], axis=1)
    act = dot(normed.reshape(seqs * rows, chans), both_weights, 1, 0)
    act = (own_mask[:, :, None] * act.reshape(seqs, rows, 2 * width)).astype(BF16)
    left = act[:, :, :width].reshape(seqs, flat)
    right = act[:, :, width:].transpose(0, 2, 1).reshape(seqs, flat)

    dma = pltpu.SemaphoreType.DMA
    shape = jax.ShapeDtypeStruct
    left_all, right_all = vmem_call(
        functools.partial(gather_kernel, dap, seq),
        (shape((seq, seqs, flat), BF16), shape((per, seq, seqs, flat), BF16)),
        [
            pltpu.VMEM((seq, seqs, flat), BF16),
            pltpu.VMEM((per, seq, seqs, flat), BF16),
            dma((seq,)), dma((seq,)), dma((dap,)), dma((per, seq)),
        ],
        2,
        0,
    )(left, right)
    left_all = left_all.reshape(all_seqs, flat)
    right_t = right_all.reshape(per, seq, seqs, width, rows).transpose(1, 2, 3, 0, 4)
    right_t = right_t.reshape(all_seqs, width * cols)
    w_dc = out_weight.reshape(width, width, chan).transpose(1, 0, 2).reshape(width * width, chan)

    groups = rows // 4
    pair_update, dl, drt, dw = vmem_call(
        main_kernel,
        (
            shape((rows, cols, chan), BF16),
            shape((all_seqs, flat), BF16),
            shape((all_seqs, width * cols), BF16),
            shape((width // 4, chan, 128), BF16),
        ),
        [
            pltpu.VMEM((groups * cols, 4 * chan), BF16),
            pltpu.VMEM((width * 128, 4 * chan), BF16),
            pltpu.VMEM((groups * cols, width * 128), BF16),
            pltpu.VMEM((width * cols, groups * 128), BF16),
        ],
        5,
    )(left_all, right_t, w_dc, cotangent, scale_t)

    dl = dl.reshape(seq, 2, half, flat).transpose(1, 0, 2, 3)
    dr = drt.reshape(seq, 2, half, width, per, rows).transpose(1, 4, 0, 2, 5, 3)
    dr = dr.reshape(2, per, seq, half, flat)
    wrows = width // 4 * chan // num
    lg, rg, wo = vmem_call(
        functools.partial(reduce_kernel, dap, seq),
        (
            shape((2, half, flat), BF16),
            shape((2, half, flat), BF16),
            shape((num, wrows, 128), BF16),
        ),
        [
            pltpu.VMEM((seq, half, flat), BF16),
            pltpu.VMEM((per, seq, half, flat), BF16),
            pltpu.VMEM((seq, half, flat), BF16),
            pltpu.VMEM((per, seq, half, flat), BF16),
            pltpu.VMEM((seq, half, flat), BF16),
            pltpu.VMEM((dap, half, flat), BF16),
            pltpu.VMEM((2, 2, half, flat), BF16),
            pltpu.VMEM((num, wrows, 128), BF16),
            pltpu.VMEM((num, wrows, 128), BF16),
            dma((3,)), dma((3,)),
            dma((seq,)), dma((seq,)),
            dma((per, seq)), dma((dap,)),
            dma((num,)), dma((num,)),
            dma((num,)), dma((num,)),
        ],
        3,
        1,
    )(dl, dr, dw.reshape(num, wrows, 128))
    grads = jnp.concatenate(
        [lg.reshape(seqs, rows, width), rg.reshape(seqs, rows, width)], axis=2
    )
    grads = (grads.astype(F32) * own_mask[:, :, None]).astype(BF16).reshape(seqs * rows, 2 * width)
    weight_part = dot(grads, normed.reshape(seqs * rows, chans), 0, 0)
    weight_total = vmem_call(
        functools.partial(total_kernel, dap, seq),
        shape((2 * width, chans), F32),
        [
            pltpu.VMEM((2 * width, chans), BF16),
            pltpu.VMEM((num, 2 * width, chans), BF16),
            dma((num,)), dma((num,)),
        ],
        1,
        2,
    )(weight_part)
    normed_grad = dot(grads, both_weights, 1, 1).reshape(seqs, rows, chans)
    _, pullback = jax.vjp(layer_norm, source)
    grad_alignment = pullback(normed_grad)[0].astype(BF16)
    wo = wo.reshape(width // 4, chan, 4, width).transpose(3, 0, 2, 1).reshape(width * width, chan)
    weight_total = weight_total.T / total_res
    return (
        pair_update,
        grad_alignment,
        weight_total[:, :width],
        weight_total[:, width:],
        wo.astype(F32) / total_res,
    )


def solution(mesh):
    placed = (
        P(("groups", "seq"), "dap", None),
        P("groups", None),
        P(("groups", "dap"), None),
        P(("groups", "dap"), "seq", "chan"),
        P(),
        P(),
        P(None, "chan"),
    )
    return jax.shard_map(
        body,
        mesh=mesh,
        in_specs=placed,
        out_specs=(
            P(("groups", "dap"), "seq", "chan"),
            P(("groups", "seq"), "dap", None),
            P("groups", None),
            P("groups", None),
            P("groups", "chan"),
        ),
        check_vma=False,
    )
```

```python
import functools

import jax
import jax.numpy as jnp
from jax import lax
from jax.experimental import pallas as pl
from jax.experimental.pallas import tpu as pltpu
from jax.sharding import PartitionSpec as P

MESH = pl.DeviceIdType.MESH
VMEM_BYTES = 48 * 1024 * 1024
F32 = jnp.float32
BF16 = jnp.bfloat16


def layer_norm(values):
    center = values - jnp.mean(values, axis=-1, keepdims=True)
    variance = jnp.mean(center * center, axis=-1, keepdims=True)
    return center * lax.rsqrt(variance + 1e-05)


def dot(a, b, ca, cb):
    return lax.dot_general(a, b, (((ca,), (cb,)), ((), ())), preferred_element_type=F32)


def vmem_call(kernel, out_shape, scratch, num_in, collective_id=None):
    params = dict(vmem_limit_bytes=VMEM_BYTES)
    if collective_id is not None:
        params.update(collective_id=collective_id, has_side_effects=True)
    return pl.pallas_call(
        kernel,
        out_shape=out_shape,
        in_specs=[pl.BlockSpec(memory_space=pltpu.VMEM)] * num_in,
        out_specs=jax.tree.map(lambda _: pl.BlockSpec(memory_space=pltpu.VMEM), out_shape),
        scratch_shapes=scratch,
        compiler_params=pltpu.CompilerParams(**params),
    )


def plane_barrier(dap, seq):
    num = dap * seq
    me = lax.axis_index("dap") * seq + lax.axis_index("seq")
    barrier = pltpu.get_barrier_semaphore()
    for step in range(1, num):
        peer = lax.rem(me + step, num)
        pl.semaphore_signal(
            barrier,
            inc=1,
            device_id={"dap": peer // seq, "seq": lax.rem(peer, seq)},
            device_id_type=MESH,
        )
    return barrier, num - 1


def arrived(buf, sem):
    pltpu.make_async_copy(buf, buf, sem).wait()


def pair_kernel(
    dap, seq, left_ref, right_ref, w_ref, cot_ref, sct_ref, pu_ref, lg_ref, rg_ref, wo_ref,
    sg, wbd, outer, dout, lall, rt, lbuf, rbuf, dl, dr, dw,
    l1, r1, l2, r2, lin, rin, pair, wrecv,
    glsend, glrecv, grsend, grrecv, csend, crecv, lsend, lrecv, rsend, rrecv, wsend, wrsem,
):
    rows, cols, chan = cot_ref.shape
    seqs, flat = left_ref.shape
    width = flat // rows
    pack = 128 // width
    groups = rows // pack
    half = seqs // 2
    per = dap // seq
    num = dap * seq
    a = lax.axis_index("dap")
    q = lax.axis_index("seq")
    h = lax.axis_index("chan")
    other = 1 - h
    me = a * seq + q
    barrier, count = plane_barrier(dap, seq)
    pl.semaphore_signal(barrier, inc=1, device_id={"chan": other}, device_id_type=MESH)
    pl.semaphore_wait(barrier, count + 1)

    def plane_copy(src, dst, send, recv, peer_a, peer_q):
        return pltpu.make_async_remote_copy(
            src_ref=src, dst_ref=dst, send_sem=send, recv_sem=recv,
            device_id={"dap": peer_a, "seq": peer_q}, device_id_type=MESH,
        )

    def core_copy(src, dst, sem):
        return pltpu.make_async_remote_copy(
            src_ref=src, dst_ref=dst, send_sem=csend.at[sem], recv_sem=crecv.at[sem],
            device_id={"chan": other}, device_id_type=MESH,
        )

    def right_copy(step):
        return plane_copy(
            right_ref, rbuf.at[lax.rem(a, per), q], grsend.at[step],
            grrecv.at[lax.rem(a, per), q], lax.rem(a + step, dap), a // per,
        )

    def left_copy(step):
        return plane_copy(
            left_ref, lbuf.at[q], glsend.at[step], glrecv.at[q], a, lax.rem(q + step, seq)
        )

    own = a // per == q
    for step in range(1, dap):
        right_copy(step).start()
    pl.when(jnp.logical_not(own))(lambda: right_copy(0).start())
    for step in range(1, seq):
        left_copy(step).start()

    for g in range(groups):
        parts = [
            cot_ref[g * pack + k].astype(F32) * sct_ref[:, g * pack + k : g * pack + k + 1]
            for k in range(pack)
        ]
        sg[g * cols : (g + 1) * cols, :] = jnp.concatenate(parts, axis=1).astype(BF16)
    row_part = lax.broadcasted_iota(jnp.int32, (128, pack * chan), 0) // width
    lane_part = lax.broadcasted_iota(jnp.int32, (128, pack * chan), 1) // chan
    diagonal = (row_part == lane_part).astype(F32).astype(BF16)
    for d in range(width):
        block = w_ref[d * width : (d + 1) * width, :]
        block = jnp.concatenate([block] * pack, axis=1)
        wbd[d * 128 : (d + 1) * 128, :] = jnp.concatenate([block] * pack, axis=0) * diagonal
    for ch in range(width // 8):
        piece = dot(sg[...], wbd[ch * 1024 : (ch + 1) * 1024, :], 1, 1)
        for dd in range(0, 8, 2):
            for block in range(per):
                at = (block * width + ch * 8 + dd) * rows
                for g in range(groups):
                    start = g * cols + block * rows
                    dout[at : at + 2 * rows, g * 128 : (g + 1) * 128] = jnp.concatenate(
                        [
                            piece[start : start + rows, e * 128 : (e + 1) * 128]
                            for e in (dd, dd + 1)
                        ],
                        axis=0,
                    ).astype(BF16)

    for src_q in range(seq):
        at = src_q * seqs

        @pl.when(src_q != q)
        def _():
            arrived(lbuf.at[src_q], glrecv.at[src_q])
            lall[at : at + seqs, :] = lbuf[src_q]

        @pl.when(src_q == q)
        def _():
            lall[at : at + seqs, :] = left_ref[...]

        for block in range(per):
            mine = jnp.logical_and(q * per + block == a, src_q == q)

            @pl.when(jnp.logical_not(mine))
            def _():
                arrived(rbuf.at[block, src_q], grrecv.at[block, src_q])
                rt[at : at + seqs, block * flat : (block + 1) * flat] = rbuf[block, src_q]

            @pl.when(mine)
            def _():
                rt[at : at + seqs, block * flat : (block + 1) * flat] = right_ref[...]

    right_part = dot(lall[...], dout[...], 1, 1).astype(BF16)
    for dest_q in range(seq):
        for core in range(2):
            at = dest_q * seqs + core * half
            for block in range(per):
                dr[core, block, dest_q] = right_part[
                    at : at + half, block * flat : (block + 1) * flat
                ]
    right_core = core_copy(dr.at[other], r1, 1)
    right_core.start()
    left_part = dot(rt[...], dout[...], 1, 0).astype(BF16)
    for dest_q in range(seq):
        for core in range(2):
            at = dest_q * seqs + core * half
            dl[core, dest_q] = left_part[at : at + half, :]
    left_core = core_copy(dl.at[other], l1, 0)
    left_core.start()

    for ch in range(width // 16):
        pieces = []
        for block in range(per):
            at = (block * width + ch * 16) * rows
            pieces.append(dot(rt[:, at : at + 16 * rows], lall[...], 0, 0))
        for dd in range(16):
            at = (ch * 16 + dd) * 128
            for g in range(groups):
                outer[g * cols : (g + 1) * cols, at : at + 128] = jnp.concatenate(
                    [
                        piece[dd * rows : (dd + 1) * rows, g * 128 : (g + 1) * 128]
                        for piece in pieces
                    ],
                    axis=0,
                ).astype(BF16)

    def left_out(dest_q):
        return plane_copy(l2.at[dest_q], lin.at[q], lsend.at[dest_q], lrecv.at[q], a, dest_q)

    def right_out(block, dest_q):
        return plane_copy(
            r2.at[block, dest_q], rin.at[a], rsend.at[block, dest_q], rrecv.at[a],
            q * per + block, dest_q,
        )

    def is_me(block, dest_q):
        return jnp.logical_and(q * per + block == a, dest_q == q)

    right_core.wait()
    for block in range(per):
        for dest_q in range(seq):
            r2[block, dest_q] = (
                dr[h, block, dest_q].astype(F32) + r1[block, dest_q].astype(F32)
            ).astype(BF16)

            @pl.when(jnp.logical_not(is_me(block, dest_q)))
            def _():
                right_out(block, dest_q).start()

    left_core.wait()
    for dest_q in range(seq):
        l2[dest_q] = (dl[h, dest_q].astype(F32) + l1[dest_q].astype(F32)).astype(BF16)

        @pl.when(dest_q != q)
        def _():
            left_out(dest_q).start()

    lane_of = lax.broadcasted_iota(jnp.int32, (chan, 128), 1) // width
    wrows = dw.shape[1]
    for ch in range(width // pack):
        wide = dot(sg[...], outer[:, ch * pack * 128 : (ch + 1) * pack * 128], 0, 0)
        total = jnp.zeros((chan, 128), F32)
        for d in range(pack):
            part = jnp.zeros((chan, 128), F32)
            for k in range(pack):
                part = jnp.where(
                    lane_of == k,
                    wide[k * chan : (k + 1) * chan, d * 128 : (d + 1) * 128],
                    part,
                )
            part = part + pltpu.roll(part, 64, 1)
            part = part + pltpu.roll(part, 32, 1)
            total = jnp.where(lane_of == d, part, total)
        pieces = chan // wrows
        for p in range(pieces):
            dw[ch * pieces + p] = total[p * wrows : (p + 1) * wrows].astype(BF16)

    def scatter(step):
        peer = lax.rem(me + step, num)
        return plane_copy(
            dw.at[peer], wrecv.at[step], wsend.at[step], wrsem.at[step],
            peer // seq, lax.rem(peer, seq),
        )

    for step in range(1, num):
        scatter(step).start()

    projected = dot(outer[...], wbd[...], 1, 0)
    for g in range(groups):
        for k in range(pack):
            i = g * pack + k
            pu_ref[i] = (
                projected[g * cols : (g + 1) * cols, k * chan : (k + 1) * chan]
                * sct_ref[:, i : i + 1]
            ).astype(BF16)

    left_sum = l2[q].astype(F32)
    for step in range(1, seq):
        src_q = lax.rem(q + step, seq)
        arrived(lin.at[src_q], lrecv.at[src_q])
        left_sum = left_sum + lin[src_q].astype(F32)
    pair[h, 0] = left_sum.astype(BF16)

    @pl.when(own)
    def _():
        rin[a] = r2[lax.rem(a, per), q]

    @pl.when(jnp.logical_not(own))
    def _():
        arrived(rin.at[a], rrecv.at[a])

    right_sum = rin[a].astype(F32)
    for step in range(1, dap):
        src_a = lax.rem(a + step, dap)
        arrived(rin.at[src_a], rrecv.at[src_a])
        right_sum = right_sum + rin[src_a].astype(F32)
    pair[h, 1] = right_sum.astype(BF16)
    final = core_copy(pair.at[h], pair.at[h], 2)
    final.start()

    wo_sum = dw[me].astype(F32)
    for step in range(1, num):
        arrived(wrecv.at[step], wrsem.at[step])
        wo_sum = wo_sum + wrecv[step].astype(F32)
    wo_ref[...] = wo_sum.astype(BF16)

    final.wait_send()
    arrived(pair.at[other], crecv.at[2])
    for core in range(2):
        lg_ref[core * half : (core + 1) * half, :] = pair[core, 0]
        rg_ref[core * half : (core + 1) * half, :] = pair[core, 1]

    for step in range(1, dap):
        right_copy(step).wait_send()
    pl.when(jnp.logical_not(own))(lambda: right_copy(0).wait_send())
    for step in range(1, seq):
        left_copy(step).wait_send()
    for step in range(1, num):
        scatter(step).wait_send()
    for dest_q in range(seq):

        @pl.when(dest_q != q)
        def _():
            left_out(dest_q).wait_send()

        for block in range(per):

            @pl.when(jnp.logical_not(is_me(block, dest_q)))
            def _():
                right_out(block, dest_q).wait_send()


def finish_kernel(
    dap, seq, total_res, grads_ref, normed_ref, source_ref, weight_ref, wo_ref,
    ga_ref, wl_ref, wr_ref, wog_ref,
    part, inbox, sums, wall, send, recv, gsend, grecv, csend, crecv,
):
    num = dap * seq
    width = wl_ref.shape[1]
    chan = wog_ref.shape[1]
    pack = 128 // width
    h = lax.axis_index("chan")
    other = 1 - h
    me = lax.axis_index("dap") * seq + lax.axis_index("seq")
    barrier, count = plane_barrier(dap, seq)
    pl.semaphore_signal(barrier, inc=1, device_id={"chan": other}, device_id_type=MESH)
    products = dot(grads_ref[...], normed_ref[...], 0, 0).astype(BF16)
    for core in range(2):
        part[core] = products[core * width : (core + 1) * width]
    wall[me] = wo_ref[...]
    pl.semaphore_wait(barrier, count + 1)

    def plane_copy(src, dst, send_sem, recv_sem, step):
        peer = lax.rem(me + step, num)
        return pltpu.make_async_remote_copy(
            src_ref=src, dst_ref=dst, send_sem=send_sem, recv_sem=recv_sem,
            device_id={"dap": peer // seq, "seq": lax.rem(peer, seq)}, device_id_type=MESH,
        )

    def part_copy(step):
        return plane_copy(part.at[h], inbox.at[step], send.at[step], recv.at[step], step)

    def wo_copy(step):
        return plane_copy(wall.at[me], wall.at[me], gsend.at[step], grecv.at[me], step)

    for step in range(1, num):
        part_copy(step).start()
    for step in range(1, num):
        wo_copy(step).start()

    values = source_ref[...].astype(F32)
    center = values - jnp.mean(values, axis=-1, keepdims=True)
    spread = lax.rsqrt(jnp.mean(center * center, axis=-1, keepdims=True) + 1e-05)
    normal = center * spread
    grad = dot(grads_ref[...], weight_ref[...], 1, 1)
    along = jnp.mean(grad * normal, axis=-1, keepdims=True)
    level = jnp.mean(grad, axis=-1, keepdims=True)
    ga_ref[...] = (spread * (grad - level - normal * along)).astype(BF16)

    inbox[0] = part[h]
    for step in range(1, num):
        part_copy(step).wait()
    total = jnp.zeros(sums.shape[1:], F32)
    for source in range(num):
        total = total + inbox[lax.rem(me - source + num, num)].astype(F32)
    sums[h] = total / total_res
    exchange = pltpu.make_async_remote_copy(
        src_ref=sums.at[h], dst_ref=sums.at[h], send_sem=csend, recv_sem=crecv,
        device_id={"chan": other}, device_id_type=MESH,
    )
    exchange.start()
    for step in range(1, num):
        src = lax.rem(me + step, num)
        arrived(wall.at[src], grecv.at[src])
    pieces = num * pack // width
    for ch in range(width // pack):
        tall = jnp.concatenate(
            [wall[ch * pieces + p].astype(F32) for p in range(pieces)], axis=0
        ).T / total_res
        for d in range(pack):
            wog_ref[pl.ds(ch * pack + d, width, stride=width), :] = tall[
                d * width : (d + 1) * width, :
            ]
    exchange.wait_send()
    arrived(sums.at[other], crecv)
    wl_ref[...] = sums[0].T
    wr_ref[...] = sums[1].T
    for step in range(1, num):
        wo_copy(step).wait_send()


def body(alignment, align_mask, pair_mask, cotangent, left_weight, right_weight, out_weight):
    seqs, rows, chans = alignment.shape
    width = left_weight.shape[1]
    chan = out_weight.shape[1]
    dap, seq = lax.axis_size("dap"), lax.axis_size("seq")
    per, num = dap // seq, dap * seq
    total_res, all_seqs = rows * dap, seqs * seq
    cols = total_res // seq
    a, q = lax.axis_index("dap"), lax.axis_index("seq")
    half = seqs // 2
    flat = rows * width

    mask_bf = align_mask.astype(BF16)
    own_mask = lax.dynamic_slice(align_mask, (q * seqs, a * rows), (seqs, rows)).astype(F32)
    mask_rows = lax.dynamic_slice_in_dim(mask_bf, a * rows, rows, 1)
    mask_cols = lax.dynamic_slice_in_dim(mask_bf, q * cols, cols, 1)
    counts = dot(mask_cols, mask_rows, 0, 0)
    own_pairs = lax.dynamic_slice_in_dim(pair_mask, q * cols, cols, 1)
    scale_t = own_pairs.T.astype(F32) / (counts + 0.001)

    normed = layer_norm(alignment.astype(F32)).astype(BF16).reshape(seqs * rows, chans)
    both_weights = jnp.concatenate([left_weight, right_weight], axis=1)
    act = dot(normed, both_weights, 1, 0)
    act = (own_mask[:, :, None] * act.reshape(seqs, rows, 2 * width)).astype(BF16)
    left = act[:, :, :width].reshape(seqs, flat)
    right = act[:, :, width:].transpose(0, 2, 1).reshape(seqs, flat)
    w_dc = out_weight.reshape(width, width, chan).transpose(1, 0, 2).reshape(width * width, chan)

    dma = pltpu.SemaphoreType.DMA
    shape = jax.ShapeDtypeStruct
    groups = rows // 4
    wrows = width // 4 * chan // num

    def room(*dims):
        return pltpu.VMEM(dims, BF16)

    pair_update, lg, rg, wo = vmem_call(
        functools.partial(pair_kernel, dap, seq),
        (
            shape((rows, cols, chan), BF16),
            shape((seqs, flat), BF16),
            shape((seqs, flat), BF16),
            shape((wrows, 128), BF16),
        ),
        [
            room(groups * cols, 4 * chan),
            room(width * 128, 4 * chan),
            room(groups * cols, width * 128),
            room(width * cols, groups * 128),
            room(all_seqs, flat),
            room(all_seqs, width * cols),
            room(seq, seqs, flat),
            room(per, seq, seqs, flat),
            room(2, seq, half, flat),
            room(2, per, seq, half, flat),
            room(num, wrows, 128),
            room(seq, half, flat),
            room(per, seq, half, flat),
            room(seq, half, flat),
            room(per, seq, half, flat),
            room(seq, half, flat),
            room(dap, half, flat),
            room(2, 2, half, flat),
            room(num, wrows, 128),
            dma((seq,)), dma((seq,)), dma((dap,)), dma((per, seq)),
            dma((3,)), dma((3,)),
            dma((seq,)), dma((seq,)),
            dma((per, seq)), dma((dap,)),
            dma((num,)), dma((num,)),
        ],
        5,
        0,
    )(left, right, w_dc, cotangent, scale_t)

    grads = jnp.concatenate(
        [lg.reshape(seqs, rows, width), rg.reshape(seqs, width, rows).transpose(0, 2, 1)], axis=2
    )
    grads = (grads.astype(F32) * own_mask[:, :, None]).astype(BF16).reshape(seqs * rows, 2 * width)
    grad_alignment, wl, wr, wog = vmem_call(
        functools.partial(finish_kernel, dap, seq, total_res),
        (
            shape((seqs * rows, chans), BF16),
            shape((chans, width), F32),
            shape((chans, width), F32),
            shape((width * width, chan), F32),
        ),
        [
            room(2, width, chans),
            room(num, width, chans),
            pltpu.VMEM((2, width, chans), F32),
            room(num, wrows, 128),
            dma((num,)), dma((num,)), dma((num,)), dma((num,)), dma, dma,
        ],
        5,
        1,
    )(grads, normed, alignment.reshape(seqs * rows, chans), both_weights, wo)
    return pair_update, grad_alignment.reshape(seqs, rows, chans), wl, wr, wog


def solution(mesh):
    placed = (
        P(("groups", "seq"), "dap", None),
        P("groups", None),
        P(("groups", "dap"), None),
        P(("groups", "dap"), "seq", "chan"),
        P(),
        P(),
        P(None, "chan"),
    )
    return jax.shard_map(
        body,
        mesh=mesh,
        in_specs=placed,
        out_specs=(
            P(("groups", "dap"), "seq", "chan"),
            P(("groups", "seq"), "dap", None),
            P("groups", None),
            P("groups", None),
            P("groups", "chan"),
        ),
        check_vma=False,
    )
```

```python
import functools

import jax
import jax.numpy as jnp
from jax import lax
from jax.experimental import pallas as pl
from jax.experimental.pallas import tpu as pltpu
from jax.sharding import PartitionSpec as P

MESH = pl.DeviceIdType.MESH
VMEM_BYTES = 62 * 1024 * 1024
F32 = jnp.float32
BF16 = jnp.bfloat16


def dot(a, b, ca, cb):
    return lax.dot_general(a, b, (((ca,), (cb,)), ((), ())), preferred_element_type=F32)


def plane_barrier(dap, seq):
    num = dap * seq
    me = lax.axis_index("dap") * seq + lax.axis_index("seq")
    barrier = pltpu.get_barrier_semaphore()
    for step in range(1, num):
        peer = lax.rem(me + step, num)
        pl.semaphore_signal(
            barrier,
            inc=1,
            device_id={"dap": peer // seq, "seq": lax.rem(peer, seq)},
            device_id_type=MESH,
        )
    return barrier, num - 1


def arrived(buf, sem):
    pltpu.make_async_copy(buf, buf, sem).wait()


def whole_kernel(
    dap, seq, total_res,
    align_hbm, amask_hbm, pmask_hbm, cot_hbm, lw_hbm, rw_hbm, ow_hbm,
    pu_ref, ga_ref, wl_ref, wr_ref, wog_ref,
    align_ref, amask, pmask, cot_ref, lw_ref, rw_ref, ow_ref,
    normal, normed, spreads, act, mask_rows, w_cd, perm, left_ref, right_ref, wtall,
    sg, wbd, outer, dout, lall, rt, lbuf, rbuf, dl, dr, dw,
    l1, r1, l2, r2, lin, rin, pair, wrecv,
    wpart, inbox, sums, wall,
    load, glsend, glrecv, grsend, grrecv, csend, crecv, lsend, lrecv, rsend, rrecv, wsend, wrsem,
    psend, precv, asend, arecv,
):
    rows, cols, chan = cot_ref.shape
    seqs, flat = left_ref.shape
    width = flat // rows
    chans = align_ref.shape[2]
    pack = 128 // width
    groups = rows // pack
    half = seqs // 2
    per = dap // seq
    num = dap * seq
    a = lax.axis_index("dap")
    q = lax.axis_index("seq")
    h = lax.axis_index("chan")
    other = 1 - h
    me = a * seq + q
    barrier, count = plane_barrier(dap, seq)
    pl.semaphore_signal(barrier, inc=1, device_id={"chan": other}, device_id_type=MESH)
    loads = [
        pltpu.make_async_copy(src, dst, load.at[n])
        for n, (src, dst) in enumerate(
            [
                (align_hbm, align_ref), (lw_hbm, lw_ref), (rw_hbm, rw_ref), (amask_hbm, amask),
                (pmask_hbm, pmask), (cot_hbm, cot_ref), (ow_hbm, ow_ref),
            ]
        )
    ]
    for copy in loads:
        copy.start()

    column = lax.broadcasted_iota(jnp.int32, (1, flat), 1)
    d_of = (column * ((65536 + rows - 1) // rows)) >> 16
    source_of = (column - d_of * rows) * width + d_of
    perm[...] = jnp.where(
        lax.broadcasted_iota(jnp.int32, (flat, flat), 0) == source_of, 1.0, 0.0
    ).astype(BF16)

    for copy in loads[:4]:
        copy.wait()
    values = align_ref[...].astype(F32).reshape(seqs * rows, chans)
    center = values - jnp.mean(values, axis=-1, keepdims=True)
    spread = lax.rsqrt(jnp.mean(center * center, axis=-1, keepdims=True) + 1e-05)
    spreads[...] = spread
    normal[...] = center * spread
    normed[...] = normal[...].astype(BF16)
    both = jnp.concatenate([lw_ref[...], rw_ref[...]], axis=0)
    act[...] = dot(normed[...], both, 1, 1).reshape(seqs, rows, 2 * width)

    def pick(size, start):
        shape = (total_res, size)
        row = lax.broadcasted_iota(jnp.int32, shape, 0)
        lane = lax.broadcasted_iota(jnp.int32, shape, 1)
        return jnp.where(row == lane + start, 1.0, 0.0).astype(BF16)

    mask_all = amask[...].astype(F32).astype(BF16)
    row_pick = pick(rows, a * rows)
    col_pick = pick(cols, q * cols)
    mask_rows[...] = dot(mask_all, row_pick, 1, 0)
    own_mask = mask_rows[pl.ds(pl.multiple_of(q * seqs, seqs), seqs), :]
    masks = [own_mask[:, i : i + 1] for i in range(rows)]
    for g in range(groups):
        parts = [act[:, i, :] * masks[i] for i in range(g * pack, (g + 1) * pack)]
        left_ref[:, g * 128 : (g + 1) * 128] = jnp.concatenate(
            [p[:, :width] for p in parts], axis=1
        ).astype(BF16)
        right_ref[:, g * 128 : (g + 1) * 128] = jnp.concatenate(
            [p[:, width:] for p in parts], axis=1
        ).astype(BF16)
    right_ref[...] = dot(right_ref[...], perm[...], 1, 0).astype(BF16)
    pl.semaphore_wait(barrier, count + 1)

    def plane_copy(src, dst, send, recv, peer_a, peer_q):
        return pltpu.make_async_remote_copy(
            src_ref=src, dst_ref=dst, send_sem=send, recv_sem=recv,
            device_id={"dap": peer_a, "seq": peer_q}, device_id_type=MESH,
        )

    def core_copy(src, dst, sem):
        return pltpu.make_async_remote_copy(
            src_ref=src, dst_ref=dst, send_sem=csend.at[sem], recv_sem=crecv.at[sem],
            device_id={"chan": other}, device_id_type=MESH,
        )

    def right_copy(step):
        return plane_copy(
            right_ref, rbuf.at[lax.rem(a, per), q], grsend.at[step],
            grrecv.at[lax.rem(a, per), q], lax.rem(a + step, dap), a // per,
        )

    def left_copy(step):
        return plane_copy(
            left_ref, lbuf.at[q], glsend.at[step], glrecv.at[q], a, lax.rem(q + step, seq)
        )

    own = a // per == q
    for step in range(1, dap):
        right_copy(step).start()
    pl.when(jnp.logical_not(own))(lambda: right_copy(0).start())
    for step in range(1, seq):
        left_copy(step).start()

    mask_cols = dot(mask_all, col_pick, 1, 0).astype(BF16)
    counts = dot(mask_cols, mask_rows[...].astype(BF16), 0, 0)
    for copy in loads[4:]:
        copy.wait()
    own_pairs = dot(col_pick, pmask[...].astype(F32).astype(BF16), 0, 1)
    scale = own_pairs / (counts + 0.001)
    w_cd[...] = ow_ref[...].astype(F32).T
    for g in range(groups):
        parts = [
            cot_ref[g * pack + k].astype(F32) * scale[:, g * pack + k : g * pack + k + 1]
            for k in range(pack)
        ]
        sg[g * cols : (g + 1) * cols, :] = jnp.concatenate(parts, axis=1).astype(BF16)
    row_part = lax.broadcasted_iota(jnp.int32, (128, pack * chan), 0) // width
    lane_part = lax.broadcasted_iota(jnp.int32, (128, pack * chan), 1) // chan
    diagonal = (row_part == lane_part).astype(F32).astype(BF16)
    for d in range(width):
        block = w_cd[pl.ds(d, width, stride=width), :].astype(BF16)
        block = jnp.concatenate([block] * pack, axis=1)
        wbd[d * 128 : (d + 1) * 128, :] = jnp.concatenate([block] * pack, axis=0) * diagonal
    for ch in range(width // 8):
        piece = dot(sg[...], wbd[ch * 1024 : (ch + 1) * 1024, :], 1, 1)
        for dd in range(0, 8, 2):
            for block in range(per):
                at = (block * width + ch * 8 + dd) * rows
                for g in range(groups):
                    start = g * cols + block * rows
                    dout[at : at + 2 * rows, g * 128 : (g + 1) * 128] = jnp.concatenate(
                        [
                            piece[start : start + rows, e * 128 : (e + 1) * 128]
                            for e in (dd, dd + 1)
                        ],
                        axis=0,
                    ).astype(BF16)

    for src_q in range(seq):
        at = src_q * seqs

        @pl.when(src_q != q)
        def _():
            arrived(lbuf.at[src_q], glrecv.at[src_q])
            lall[at : at + seqs, :] = lbuf[src_q]

        @pl.when(src_q == q)
        def _():
            lall[at : at + seqs, :] = left_ref[...]

        for block in range(per):
            mine = jnp.logical_and(q * per + block == a, src_q == q)

            @pl.when(jnp.logical_not(mine))
            def _():
                arrived(rbuf.at[block, src_q], grrecv.at[block, src_q])
                rt[at : at + seqs, block * flat : (block + 1) * flat] = rbuf[block, src_q]

            @pl.when(mine)
            def _():
                rt[at : at + seqs, block * flat : (block + 1) * flat] = right_ref[...]

    right_part = dot(lall[...], dout[...], 1, 1).astype(BF16)
    for dest_q in range(seq):
        for core in range(2):
            at = dest_q * seqs + core * half
            for block in range(per):
                dr[core, block, dest_q] = right_part[
                    at : at + half, block * flat : (block + 1) * flat
                ]
    right_core = core_copy(dr.at[other], r1, 1)
    right_core.start()
    left_part = dot(rt[...], dout[...], 1, 0).astype(BF16)
    for dest_q in range(seq):
        for core in range(2):
            at = dest_q * seqs + core * half
            dl[core, dest_q] = left_part[at : at + half, :]
    left_core = core_copy(dl.at[other], l1, 0)
    left_core.start()

    for ch in range(width // 16):
        pieces = []
        for block in range(per):
            at = (block * width + ch * 16) * rows
            pieces.append(dot(rt[:, at : at + 16 * rows], lall[...], 0, 0))
        for dd in range(16):
            at = (ch * 16 + dd) * 128
            for g in range(groups):
                outer[g * cols : (g + 1) * cols, at : at + 128] = jnp.concatenate(
                    [
                        piece[dd * rows : (dd + 1) * rows, g * 128 : (g + 1) * 128]
                        for piece in pieces
                    ],
                    axis=0,
                ).astype(BF16)

    def left_out(dest_q):
        return plane_copy(l2.at[dest_q], lin.at[q], lsend.at[dest_q], lrecv.at[q], a, dest_q)

    def right_out(block, dest_q):
        return plane_copy(
            r2.at[block, dest_q], rin.at[a], rsend.at[block, dest_q], rrecv.at[a],
            q * per + block, dest_q,
        )

    def is_me(block, dest_q):
        return jnp.logical_and(q * per + block == a, dest_q == q)

    right_core.wait()
    for block in range(per):
        for dest_q in range(seq):
            r2[block, dest_q] = (
                dr[h, block, dest_q].astype(F32) + r1[block, dest_q].astype(F32)
            ).astype(BF16)

            @pl.when(jnp.logical_not(is_me(block, dest_q)))
            def _():
                right_out(block, dest_q).start()

    left_core.wait()
    for dest_q in range(seq):
        l2[dest_q] = (dl[h, dest_q].astype(F32) + l1[dest_q].astype(F32)).astype(BF16)

        @pl.when(dest_q != q)
        def _():
            left_out(dest_q).start()

    lane_of = lax.broadcasted_iota(jnp.int32, (chan, 128), 1) // width
    wrows = dw.shape[1]
    for ch in range(width // pack):
        wide = dot(sg[...], outer[:, ch * pack * 128 : (ch + 1) * pack * 128], 0, 0)
        total = jnp.zeros((chan, 128), F32)
        for d in range(pack):
            part = jnp.zeros((chan, 128), F32)
            for k in range(pack):
                part = jnp.where(
                    lane_of == k,
                    wide[k * chan : (k + 1) * chan, d * 128 : (d + 1) * 128],
                    part,
                )
            part = part + pltpu.roll(part, 64, 1)
            part = part + pltpu.roll(part, 32, 1)
            total = jnp.where(lane_of == d, part, total)
        pieces = chan // wrows
        for p in range(pieces):
            dw[ch * pieces + p] = total[p * wrows : (p + 1) * wrows].astype(BF16)

    def scatter(step):
        peer = lax.rem(me + step, num)
        return plane_copy(
            dw.at[peer], wrecv.at[step], wsend.at[step], wrsem.at[step],
            peer // seq, lax.rem(peer, seq),
        )

    for step in range(1, num):
        scatter(step).start()

    projected = dot(outer[...], wbd[...], 1, 0)
    for g in range(groups):
        for k in range(pack):
            i = g * pack + k
            pu_ref[i] = (
                projected[g * cols : (g + 1) * cols, k * chan : (k + 1) * chan]
                * scale[:, i : i + 1]
            ).astype(BF16)

    left_sum = l2[q].astype(F32)
    for step in range(1, seq):
        src_q = lax.rem(q + step, seq)
        arrived(lin.at[src_q], lrecv.at[src_q])
        left_sum = left_sum + lin[src_q].astype(F32)
    pair[h, 0] = left_sum.astype(BF16)

    @pl.when(own)
    def _():
        rin[a] = r2[lax.rem(a, per), q]

    @pl.when(jnp.logical_not(own))
    def _():
        arrived(rin.at[a], rrecv.at[a])

    right_sum = rin[a].astype(F32)
    for step in range(1, dap):
        src_a = lax.rem(a + step, dap)
        arrived(rin.at[src_a], rrecv.at[src_a])
        right_sum = right_sum + rin[src_a].astype(F32)
    pair[h, 1] = right_sum.astype(BF16)
    final = core_copy(pair.at[h], pair.at[h], 2)
    final.start()

    wo_sum = dw[me].astype(F32)
    for step in range(1, num):
        arrived(wrecv.at[step], wrsem.at[step])
        wo_sum = wo_sum + wrecv[step].astype(F32)
    wall[me] = wo_sum.astype(BF16)

    def peer_copy(src, dst, send, recv, step):
        peer = lax.rem(me + step, num)
        return plane_copy(src, dst, send, recv, peer // seq, lax.rem(peer, seq))

    def part_copy(step):
        return peer_copy(wpart.at[h], inbox.at[step], psend.at[step], precv.at[step], step)

    def wo_copy(step):
        return peer_copy(wall.at[me], wall.at[me], asend.at[step], arecv.at[me], step)

    for step in range(1, num):
        wo_copy(step).start()

    final.wait_send()
    arrived(pair.at[other], crecv.at[2])
    left_grad = jnp.concatenate([pair[0, 0], pair[1, 0]], axis=0).astype(F32)
    right_grad = jnp.concatenate([pair[0, 1], pair[1, 1]], axis=0)
    right_grad = dot(right_grad, perm[...], 1, 1)
    for i in range(rows):
        lanes = slice(i * width, (i + 1) * width)
        act[:, i, :] = (
            jnp.concatenate([left_grad[:, lanes], right_grad[:, lanes]], axis=1) * masks[i]
        )
    grads = act[...].reshape(seqs * rows, 2 * width).astype(BF16)

    products = dot(grads, normed[...], 0, 0).astype(BF16)
    for core in range(2):
        wpart[core] = products[core * width : (core + 1) * width]
    for step in range(1, num):
        part_copy(step).start()
    grad = dot(grads, both, 1, 0)
    along = jnp.mean(grad * normal[...], axis=-1, keepdims=True)
    level = jnp.mean(grad, axis=-1, keepdims=True)
    ga_ref[...] = (
        (spreads[...] * (grad - level - normal[...] * along))
        .reshape(seqs, rows, chans)
        .astype(BF16)
    )

    for step in range(1, num):
        src = lax.rem(me + step, num)
        arrived(wall.at[src], arecv.at[src])
    pieces = num * pack // width
    for ch in range(width // pack):
        tall = jnp.concatenate(
            [wall[ch * pieces + p].astype(F32) for p in range(pieces)], axis=0
        ).T / total_res
        for d in range(pack):
            wtall[pl.ds(ch * pack + d, width, stride=width), :] = tall[
                d * width : (d + 1) * width, :
            ]
    wog_ref[...] = wtall[...].T

    inbox[0] = wpart[h]
    for step in range(1, num):
        part_copy(step).wait()
    total = jnp.zeros(sums.shape[1:], F32)
    for source in range(num):
        total = total + inbox[lax.rem(me - source + num, num)].astype(F32)
    sums[h] = total / total_res
    exchange = core_copy(sums.at[h], sums.at[h], 3)
    exchange.start()
    exchange.wait_send()
    arrived(sums.at[other], crecv.at[3])
    wl_ref[...] = sums[0]
    wr_ref[...] = sums[1]

    for step in range(1, num):
        wo_copy(step).wait_send()
    for step in range(1, dap):
        right_copy(step).wait_send()
    pl.when(jnp.logical_not(own))(lambda: right_copy(0).wait_send())
    for step in range(1, seq):
        left_copy(step).wait_send()
    for step in range(1, num):
        scatter(step).wait_send()
    for dest_q in range(seq):

        @pl.when(dest_q != q)
        def _():
            left_out(dest_q).wait_send()

        for block in range(per):

            @pl.when(jnp.logical_not(is_me(block, dest_q)))
            def _():
                right_out(block, dest_q).wait_send()


def store_kernel(*refs):
    count = (len(refs) - 1) // 2
    sems = refs[-1]
    copies = [
        pltpu.make_async_copy(refs[n], refs[count + n], sems.at[n]) for n in range(count)
    ]
    for copy in copies:
        copy.start()
    for copy in copies:
        copy.wait()


def body(alignment, align_mask, pair_mask, cotangent, left_weight, right_weight, out_weight):
    seqs, rows, chans = alignment.shape
    width = left_weight.shape[1]
    chan = out_weight.shape[1]
    dap, seq = lax.axis_size("dap"), lax.axis_size("seq")
    per, num = dap // seq, dap * seq
    total_res, all_seqs = rows * dap, seqs * seq
    cols = total_res // seq
    half = seqs // 2
    flat = rows * width
    dma = pltpu.SemaphoreType.DMA
    shape = jax.ShapeDtypeStruct
    groups = rows // 4
    wrows = width // 4 * chan // num

    def room(*dims):
        return pltpu.VMEM(dims, BF16)

    def wide(*dims):
        return pltpu.VMEM(dims, F32)

    args = (
        alignment, align_mask, pair_mask, cotangent, left_weight.T, right_weight.T, out_weight.T,
    )
    out_shape = (
        shape((rows, cols, chan), BF16),
        shape((seqs, rows, chans), BF16),
        shape((width, chans), F32),
        shape((width, chans), F32),
        shape((chan, width * width), F32),
    )
    results = pl.pallas_call(
        functools.partial(whole_kernel, dap, seq, total_res),
        out_shape=out_shape,
        in_specs=[pl.BlockSpec(memory_space=pltpu.HBM)] * len(args),
        out_specs=tuple(pl.BlockSpec(memory_space=pltpu.VMEM) for _ in out_shape),
        scratch_shapes=[pltpu.VMEM(x.shape, x.dtype) for x in args]
        + [
            wide(seqs * rows, chans),
            room(seqs * rows, chans),
            wide(seqs * rows, 1),
            wide(seqs, rows, 2 * width),
            wide(all_seqs, rows),
            wide(width * width, chan),
            room(flat, flat),
            room(seqs, flat),
            room(seqs, flat),
            wide(width * width, chan),
            room(groups * cols, 4 * chan),
            room(width * 128, 4 * chan),
            room(groups * cols, width * 128),
            room(width * cols, groups * 128),
            room(all_seqs, flat),
            room(all_seqs, width * cols),
            room(seq, seqs, flat),
            room(per, seq, seqs, flat),
            room(2, seq, half, flat),
            room(2, per, seq, half, flat),
            room(num, wrows, 128),
            room(seq, half, flat),
            room(per, seq, half, flat),
            room(seq, half, flat),
            room(per, seq, half, flat),
            room(seq, half, flat),
            room(dap, half, flat),
            room(2, 2, half, flat),
            room(num, wrows, 128),
            room(2, width, chans),
            room(num, width, chans),
            wide(2, width, chans),
            room(num, wrows, 128),
            dma((7,)),
            dma((seq,)), dma((seq,)), dma((dap,)), dma((per, seq)),
            dma((4,)), dma((4,)),
            dma((seq,)), dma((seq,)),
            dma((per, seq)), dma((dap,)),
            dma((num,)), dma((num,)),
            dma((num,)), dma((num,)),
            dma((num,)), dma((num,)),
        ],
        compiler_params=pltpu.CompilerParams(
            vmem_limit_bytes=VMEM_BYTES, collective_id=0, has_side_effects=True
        ),
    )(*args)
    pair_update, grad_alignment, wl, wr, wog = pl.pallas_call(
        store_kernel,
        out_shape=out_shape,
        in_specs=[pl.BlockSpec(memory_space=pl.ANY)] * len(results),
        out_specs=tuple(pl.BlockSpec(memory_space=pltpu.HBM) for _ in out_shape),
        scratch_shapes=[dma((len(results),))],
    )(*results)
    return pair_update, grad_alignment, wl.T, wr.T, wog.T


def solution(mesh):
    placed = (
        P(("groups", "seq"), "dap", None),
        P("groups", None),
        P(("groups", "dap"), None),
        P(("groups", "dap"), "seq", "chan"),
        P(),
        P(),
        P(None, "chan"),
    )
    return jax.shard_map(
        body,
        mesh=mesh,
        in_specs=placed,
        out_specs=(
            P(("groups", "dap"), "seq", "chan"),
            P(("groups", "seq"), "dap", None),
            P("groups", None),
            P("groups", None),
            P("groups", "chan"),
        ),
        check_vma=False,
    )
```

```python
import functools

import jax
import jax.numpy as jnp
from jax import lax
from jax.experimental import pallas as pl
from jax.experimental.pallas import tpu as pltpu
from jax.sharding import PartitionSpec as P

MESH = pl.DeviceIdType.MESH
VMEM_BYTES = 62 * 1024 * 1024
F32 = jnp.float32
BF16 = jnp.bfloat16


def dot(a, b, ca, cb):
    return lax.dot_general(a, b, (((ca,), (cb,)), ((), ())), preferred_element_type=F32)


def plane_barrier(dap, seq):
    num = dap * seq
    me = lax.axis_index("dap") * seq + lax.axis_index("seq")
    barrier = pltpu.get_barrier_semaphore()
    for step in range(1, num):
        peer = lax.rem(me + step, num)
        pl.semaphore_signal(
            barrier,
            inc=1,
            device_id={"dap": peer // seq, "seq": lax.rem(peer, seq)},
            device_id_type=MESH,
        )
    return barrier, num - 1


def arrived(buf, sem):
    pltpu.make_async_copy(buf, buf, sem).wait()


def whole_kernel(
    dap, seq, total_res,
    align_hbm, amask_hbm, pmask_hbm, cot_hbm, lw_hbm, rw_hbm, ow_hbm,
    pu_ref, ga_ref, wl_ref, wr_ref, wog_ref,
    align_ref, amask, pmask, cot_ref, lw_ref, rw_ref, ow_ref,
    normal, normed, spreads, act, mask_rows, w_cd, perm, left_ref, right_ref, wtall,
    sg, wbd, outer, dout, lall, rt, lbuf, rbuf, dl, dr, dw,
    l1, r1, l2, r2, lin, rin, pair, wrecv,
    wpart, inbox, sums, wall,
    load, glsend, glrecv, grsend, grrecv, csend, crecv, lsend, lrecv, rsend, rrecv, wsend, wrsem,
    psend, precv, asend, arecv,
):
    rows, cols, chan = cot_ref.shape
    seqs, flat = left_ref.shape
    width = flat // rows
    chans = align_ref.shape[2]
    pack = 128 // width
    groups = rows // pack
    half = seqs // 2
    per = dap // seq
    num = dap * seq
    a = lax.axis_index("dap")
    q = lax.axis_index("seq")
    h = lax.axis_index("chan")
    other = 1 - h
    me = a * seq + q
    barrier, count = plane_barrier(dap, seq)
    pl.semaphore_signal(barrier, inc=1, device_id={"chan": other}, device_id_type=MESH)
    loads = [
        pltpu.make_async_copy(src, dst, load.at[n])
        for n, (src, dst) in enumerate(
            [
                (align_hbm, align_ref), (lw_hbm, lw_ref), (rw_hbm, rw_ref), (amask_hbm, amask),
                (pmask_hbm, pmask), (cot_hbm, cot_ref), (ow_hbm, ow_ref),
            ]
        )
    ]
    for copy in loads:
        copy.start()

    column = lax.broadcasted_iota(jnp.int32, (1, flat), 1)
    d_of = (column * ((65536 + rows - 1) // rows)) >> 16
    source_of = (column - d_of * rows) * width + d_of
    perm[...] = jnp.where(
        lax.broadcasted_iota(jnp.int32, (flat, flat), 0) == source_of, 1.0, 0.0
    ).astype(BF16)

    for copy in loads[:4]:
        copy.wait()
    values = align_ref[...].astype(F32).reshape(seqs * rows, chans)
    center = values - jnp.mean(values, axis=-1, keepdims=True)
    spread = lax.rsqrt(jnp.mean(center * center, axis=-1, keepdims=True) + 1e-05)
    spreads[...] = spread
    normal[...] = center * spread
    normed[...] = normal[...].astype(BF16)
    both = jnp.concatenate([lw_ref[...], rw_ref[...]], axis=0)
    act[...] = dot(normed[...], both, 1, 1).reshape(seqs, rows, 2 * width)

    def pick(size, start):
        shape = (total_res, size)
        row = lax.broadcasted_iota(jnp.int32, shape, 0)
        lane = lax.broadcasted_iota(jnp.int32, shape, 1)
        return jnp.where(row == lane + start, 1.0, 0.0).astype(BF16)

    mask_all = amask[...].astype(F32).astype(BF16)
    row_pick = pick(rows, a * rows)
    col_pick = pick(cols, q * cols)
    mask_rows[...] = dot(mask_all, row_pick, 1, 0)
    own_mask = mask_rows[pl.ds(pl.multiple_of(q * seqs, seqs), seqs), :]
    masks = [own_mask[:, i : i + 1] for i in range(rows)]
    for g in range(groups):
        parts = [act[:, i, :] * masks[i] for i in range(g * pack, (g + 1) * pack)]
        left_ref[:, g * 128 : (g + 1) * 128] = jnp.concatenate(
            [p[:, :width] for p in parts], axis=1
        ).astype(BF16)
        right_ref[:, g * 128 : (g + 1) * 128] = jnp.concatenate(
            [p[:, width:] for p in parts], axis=1
        ).astype(BF16)
    right_ref[...] = dot(right_ref[...], perm[...], 1, 0).astype(BF16)
    pl.semaphore_wait(barrier, count + 1)

    def plane_copy(src, dst, send, recv, peer_a, peer_q):
        return pltpu.make_async_remote_copy(
            src_ref=src, dst_ref=dst, send_sem=send, recv_sem=recv,
            device_id={"dap": peer_a, "seq": peer_q}, device_id_type=MESH,
        )

    def core_copy(src, dst, sem):
        return pltpu.make_async_remote_copy(
            src_ref=src, dst_ref=dst, send_sem=csend.at[sem], recv_sem=crecv.at[sem],
            device_id={"chan": other}, device_id_type=MESH,
        )

    def right_copy(step):
        return plane_copy(
            right_ref, rbuf.at[lax.rem(a, per), q], grsend.at[step],
            grrecv.at[lax.rem(a, per), q], lax.rem(a + step, dap), a // per,
        )

    def left_copy(step):
        return plane_copy(
            left_ref, lbuf.at[q], glsend.at[step], glrecv.at[q], a, lax.rem(q + step, seq)
        )

    own = a // per == q
    for step in range(1, dap):
        right_copy(step).start()
    pl.when(jnp.logical_not(own))(lambda: right_copy(0).start())
    for step in range(1, seq):
        left_copy(step).start()

    mask_cols = dot(mask_all, col_pick, 1, 0).astype(BF16)
    counts = dot(mask_cols, mask_rows[...].astype(BF16), 0, 0)
    for copy in loads[4:]:
        copy.wait()
    own_pairs = dot(col_pick, pmask[...].astype(F32).astype(BF16), 0, 1)
    scale = own_pairs / (counts + 0.001)
    w_cd[...] = ow_ref[...].astype(F32).T
    for g in range(groups):
        parts = [
            cot_ref[g * pack + k].astype(F32) * scale[:, g * pack + k : g * pack + k + 1]
            for k in range(pack)
        ]
        sg[g * cols : (g + 1) * cols, :] = jnp.concatenate(parts, axis=1).astype(BF16)
    row_part = lax.broadcasted_iota(jnp.int32, (128, pack * chan), 0) // width
    lane_part = lax.broadcasted_iota(jnp.int32, (128, pack * chan), 1) // chan
    diagonal = (row_part == lane_part).astype(F32).astype(BF16)
    for d in range(width):
        block = w_cd[pl.ds(d, width, stride=width), :].astype(BF16)
        block = jnp.concatenate([block] * pack, axis=1)
        wbd[d * 128 : (d + 1) * 128, :] = jnp.concatenate([block] * pack, axis=0) * diagonal
    for ch in range(width // 8):
        piece = dot(sg[...], wbd[ch * 1024 : (ch + 1) * 1024, :], 1, 1)
        for dd in range(0, 8, 2):
            for block in range(per):
                at = (block * width + ch * 8 + dd) * rows
                for g in range(groups):
                    start = g * cols + block * rows
                    dout[at : at + 2 * rows, g * 128 : (g + 1) * 128] = jnp.concatenate(
                        [
                            piece[start : start + rows, e * 128 : (e + 1) * 128]
                            for e in (dd, dd + 1)
                        ],
                        axis=0,
                    ).astype(BF16)

    for src_q in range(seq):
        at = src_q * seqs

        @pl.when(src_q != q)
        def _():
            arrived(lbuf.at[src_q], glrecv.at[src_q])
            lall[at : at + seqs, :] = lbuf[src_q]

        @pl.when(src_q == q)
        def _():
            lall[at : at + seqs, :] = left_ref[...]

        for block in range(per):
            mine = jnp.logical_and(q * per + block == a, src_q == q)

            @pl.when(jnp.logical_not(mine))
            def _():
                arrived(rbuf.at[block, src_q], grrecv.at[block, src_q])
                rt[at : at + seqs, block * flat : (block + 1) * flat] = rbuf[block, src_q]

            @pl.when(mine)
            def _():
                rt[at : at + seqs, block * flat : (block + 1) * flat] = right_ref[...]

    right_part = dot(lall[...], dout[...], 1, 1).astype(BF16)
    for dest_q in range(seq):
        for core in range(2):
            at = dest_q * seqs + core * half
            for block in range(per):
                dr[core, block, dest_q] = right_part[
                    at : at + half, block * flat : (block + 1) * flat
                ]
    right_core = core_copy(dr.at[other], r1, 1)
    right_core.start()
    left_part = dot(rt[...], dout[...], 1, 0).astype(BF16)
    for dest_q in range(seq):
        for core in range(2):
            at = dest_q * seqs + core * half
            dl[core, dest_q] = left_part[at : at + half, :]
    left_core = core_copy(dl.at[other], l1, 0)
    left_core.start()

    for ch in range(width // 16):
        pieces = []
        for block in range(per):
            at = (block * width + ch * 16) * rows
            pieces.append(dot(rt[:, at : at + 16 * rows], lall[...], 0, 0))
        for dd in range(16):
            at = (ch * 16 + dd) * 128
            for g in range(groups):
                outer[g * cols : (g + 1) * cols, at : at + 128] = jnp.concatenate(
                    [
                        piece[dd * rows : (dd + 1) * rows, g * 128 : (g + 1) * 128]
                        for piece in pieces
                    ],
                    axis=0,
                ).astype(BF16)

    def left_out(dest_q):
        return plane_copy(l2.at[dest_q], lin.at[q], lsend.at[dest_q], lrecv.at[q], a, dest_q)

    def right_out(block, dest_q):
        return plane_copy(
            r2.at[block, dest_q], rin.at[a], rsend.at[block, dest_q], rrecv.at[a],
            q * per + block, dest_q,
        )

    def is_me(block, dest_q):
        return jnp.logical_and(q * per + block == a, dest_q == q)

    right_core.wait()
    for block in range(per):
        for dest_q in range(seq):
            r2[block, dest_q] = (
                dr[h, block, dest_q].astype(F32) + r1[block, dest_q].astype(F32)
            ).astype(BF16)

            @pl.when(jnp.logical_not(is_me(block, dest_q)))
            def _():
                right_out(block, dest_q).start()

    left_core.wait()
    for dest_q in range(seq):
        l2[dest_q] = (dl[h, dest_q].astype(F32) + l1[dest_q].astype(F32)).astype(BF16)

        @pl.when(dest_q != q)
        def _():
            left_out(dest_q).start()

    lane_of = lax.broadcasted_iota(jnp.int32, (chan, 128), 1) // width
    wrows = dw.shape[1]
    for ch in range(width // pack):
        wide = dot(sg[...], outer[:, ch * pack * 128 : (ch + 1) * pack * 128], 0, 0)
        total = jnp.zeros((chan, 128), F32)
        for d in range(pack):
            part = jnp.zeros((chan, 128), F32)
            for k in range(pack):
                part = jnp.where(
                    lane_of == k,
                    wide[k * chan : (k + 1) * chan, d * 128 : (d + 1) * 128],
                    part,
                )
            part = part + pltpu.roll(part, 64, 1)
            part = part + pltpu.roll(part, 32, 1)
            total = jnp.where(lane_of == d, part, total)
        pieces = chan // wrows
        for p in range(pieces):
            dw[ch * pieces + p] = total[p * wrows : (p + 1) * wrows].astype(BF16)

    def scatter(step):
        peer = lax.rem(me + step, num)
        return plane_copy(
            dw.at[peer], wrecv.at[step], wsend.at[step], wrsem.at[step],
            peer // seq, lax.rem(peer, seq),
        )

    for step in range(1, num):
        scatter(step).start()

    projected = dot(outer[...], wbd[...], 1, 0)
    for g in range(groups):
        for k in range(pack):
            i = g * pack + k
            pu_ref[i] = (
                projected[g * cols : (g + 1) * cols, k * chan : (k + 1) * chan]
                * scale[:, i : i + 1]
            ).astype(BF16)

    left_sum = l2[q].astype(F32)
    for step in range(1, seq):
        src_q = lax.rem(q + step, seq)
        arrived(lin.at[src_q], lrecv.at[src_q])
        left_sum = left_sum + lin[src_q].astype(F32)
    pair[h, 0] = left_sum.astype(BF16)

    @pl.when(own)
    def _():
        rin[a] = r2[lax.rem(a, per), q]

    @pl.when(jnp.logical_not(own))
    def _():
        arrived(rin.at[a], rrecv.at[a])

    right_sum = rin[a].astype(F32)
    for step in range(1, dap):
        src_a = lax.rem(a + step, dap)
        arrived(rin.at[src_a], rrecv.at[src_a])
        right_sum = right_sum + rin[src_a].astype(F32)
    pair[h, 1] = right_sum.astype(BF16)
    final = core_copy(pair.at[h], pair.at[h], 2)
    final.start()

    wo_sum = dw[me].astype(F32)
    for step in range(1, num):
        arrived(wrecv.at[step], wrsem.at[step])
        wo_sum = wo_sum + wrecv[step].astype(F32)
    wall[me] = wo_sum.astype(BF16)

    def peer_copy(src, dst, send, recv, step):
        peer = lax.rem(me + step, num)
        return plane_copy(src, dst, send, recv, peer // seq, lax.rem(peer, seq))

    def part_copy(step):
        return peer_copy(wpart.at[h], inbox.at[step], psend.at[step], precv.at[step], step)

    def wo_copy(step):
        return peer_copy(wall.at[me], wall.at[me], asend.at[step], arecv.at[me], step)

    for step in range(1, num):
        wo_copy(step).start()

    final.wait_send()
    arrived(pair.at[other], crecv.at[2])
    left_grad = jnp.concatenate([pair[0, 0], pair[1, 0]], axis=0).astype(F32)
    right_grad = jnp.concatenate([pair[0, 1], pair[1, 1]], axis=0)
    right_grad = dot(right_grad, perm[...], 1, 1)
    for i in range(rows):
        lanes = slice(i * width, (i + 1) * width)
        act[:, i, :] = (
            jnp.concatenate([left_grad[:, lanes], right_grad[:, lanes]], axis=1) * masks[i]
        )
    grads = act[...].reshape(seqs * rows, 2 * width).astype(BF16)

    products = dot(grads, normed[...], 0, 0).astype(BF16)
    for core in range(2):
        wpart[core] = products[core * width : (core + 1) * width]
    for step in range(1, num):
        part_copy(step).start()
    grad = dot(grads, both, 1, 0)
    along = jnp.mean(grad * normal[...], axis=-1, keepdims=True)
    level = jnp.mean(grad, axis=-1, keepdims=True)
    ga_ref[...] = (
        (spreads[...] * (grad - level - normal[...] * along))
        .reshape(seqs, rows, chans)
        .astype(BF16)
    )

    for step in range(1, num):
        src = lax.rem(me + step, num)
        arrived(wall.at[src], arecv.at[src])
    pieces = num * pack // width
    for ch in range(width // pack):
        tall = jnp.concatenate(
            [wall[ch * pieces + p].astype(F32) for p in range(pieces)], axis=0
        ).T / total_res
        for d in range(pack):
            wtall[pl.ds(ch * pack + d, width, stride=width), :] = tall[
                d * width : (d + 1) * width, :
            ]
    wog_ref[...] = wtall[...].T

    inbox[0] = wpart[h]
    for step in range(1, num):
        part_copy(step).wait()
    total = jnp.zeros(sums.shape[1:], F32)
    for source in range(num):
        total = total + inbox[lax.rem(me - source + num, num)].astype(F32)
    sums[h] = total / total_res
    exchange = core_copy(sums.at[h], sums.at[h], 3)
    exchange.start()
    exchange.wait_send()
    arrived(sums.at[other], crecv.at[3])
    wl_ref[...] = sums[0]
    wr_ref[...] = sums[1]

    for step in range(1, num):
        wo_copy(step).wait_send()
    for step in range(1, dap):
        right_copy(step).wait_send()
    pl.when(jnp.logical_not(own))(lambda: right_copy(0).wait_send())
    for step in range(1, seq):
        left_copy(step).wait_send()
    for step in range(1, num):
        scatter(step).wait_send()
    for dest_q in range(seq):

        @pl.when(dest_q != q)
        def _():
            left_out(dest_q).wait_send()

        for block in range(per):

            @pl.when(jnp.logical_not(is_me(block, dest_q)))
            def _():
                right_out(block, dest_q).wait_send()


def store_kernel(*refs):
    count = (len(refs) - 2) // 3
    sources, dests, rooms = (refs[n * count : (n + 1) * count] for n in range(3))
    in_sems, out_sems = refs[-2:]
    ins = [pltpu.make_async_copy(sources[n], rooms[n], in_sems.at[n]) for n in range(count)]
    outs = [pltpu.make_async_copy(rooms[n], dests[n], out_sems.at[n]) for n in range(count)]
    for copy in ins:
        copy.start()
    for n in range(count):
        ins[n].wait()
        outs[n].start()
    for copy in outs:
        copy.wait()


def body(alignment, align_mask, pair_mask, cotangent, left_weight, right_weight, out_weight):
    seqs, rows, chans = alignment.shape
    width = left_weight.shape[1]
    chan = out_weight.shape[1]
    dap, seq = lax.axis_size("dap"), lax.axis_size("seq")
    per, num = dap // seq, dap * seq
    total_res, all_seqs = rows * dap, seqs * seq
    cols = total_res // seq
    half = seqs // 2
    flat = rows * width
    dma = pltpu.SemaphoreType.DMA
    shape = jax.ShapeDtypeStruct
    groups = rows // 4
    wrows = width // 4 * chan // num

    def room(*dims):
        return pltpu.VMEM(dims, BF16)

    def wide(*dims):
        return pltpu.VMEM(dims, F32)

    args = (
        alignment, align_mask, pair_mask, cotangent, left_weight.T, right_weight.T, out_weight.T,
    )
    out_shape = (
        shape((rows, cols, chan), BF16),
        shape((seqs, rows, chans), BF16),
        shape((width, chans), F32),
        shape((width, chans), F32),
        shape((chan, width * width), F32),
    )
    results = pl.pallas_call(
        functools.partial(whole_kernel, dap, seq, total_res),
        out_shape=out_shape,
        in_specs=[pl.BlockSpec(memory_space=pltpu.HBM)] * len(args),
        out_specs=tuple(pl.BlockSpec(memory_space=pltpu.VMEM) for _ in out_shape),
        scratch_shapes=[pltpu.VMEM(x.shape, x.dtype) for x in args]
        + [
            wide(seqs * rows, chans),
            room(seqs * rows, chans),
            wide(seqs * rows, 1),
            wide(seqs, rows, 2 * width),
            wide(all_seqs, rows),
            wide(width * width, chan),
            room(flat, flat),
            room(seqs, flat),
            room(seqs, flat),
            wide(width * width, chan),
            room(groups * cols, 4 * chan),
            room(width * 128, 4 * chan),
            room(groups * cols, width * 128),
            room(width * cols, groups * 128),
            room(all_seqs, flat),
            room(all_seqs, width * cols),
            room(seq, seqs, flat),
            room(per, seq, seqs, flat),
            room(2, seq, half, flat),
            room(2, per, seq, half, flat),
            room(num, wrows, 128),
            room(seq, half, flat),
            room(per, seq, half, flat),
            room(seq, half, flat),
            room(per, seq, half, flat),
            room(seq, half, flat),
            room(dap, half, flat),
            room(2, 2, half, flat),
            room(num, wrows, 128),
            room(2, width, chans),
            room(num, width, chans),
            wide(2, width, chans),
            room(num, wrows, 128),
            dma((7,)),
            dma((seq,)), dma((seq,)), dma((dap,)), dma((per, seq)),
            dma((4,)), dma((4,)),
            dma((seq,)), dma((seq,)),
            dma((per, seq)), dma((dap,)),
            dma((num,)), dma((num,)),
            dma((num,)), dma((num,)),
            dma((num,)), dma((num,)),
        ],
        compiler_params=pltpu.CompilerParams(
            vmem_limit_bytes=VMEM_BYTES, collective_id=0, has_side_effects=True
        ),
    )(*args)
    pair_update, grad_alignment, wl, wr, wog = pl.pallas_call(
        store_kernel,
        out_shape=out_shape,
        in_specs=[pl.BlockSpec(memory_space=pltpu.HBM)] * len(results),
        out_specs=tuple(pl.BlockSpec(memory_space=pltpu.HBM) for _ in out_shape),
        scratch_shapes=[pltpu.VMEM(x.shape, x.dtype) for x in out_shape]
        + [dma((len(results),)), dma((len(results),))],
        compiler_params=pltpu.CompilerParams(vmem_limit_bytes=VMEM_BYTES),
    )(*results)
    return pair_update, grad_alignment, wl.T, wr.T, wog.T


def solution(mesh):
    placed = (
        P(("groups", "seq"), "dap", None),
        P("groups", None),
        P(("groups", "dap"), None),
        P(("groups", "dap"), "seq", "chan"),
        P(),
        P(),
        P(None, "chan"),
    )
    return jax.shard_map(
        body,
        mesh=mesh,
        in_specs=placed,
        out_specs=(
            P(("groups", "dap"), "seq", "chan"),
            P(("groups", "seq"), "dap", None),
            P("groups", None),
            P("groups", None),
            P("groups", "chan"),
        ),
        check_vma=False,
    )
```
